32 devices in a mesh: pix: 8 (over z, y), tm: 4 (over x, core).
Axes of the slice: x: 2, y: 2, z: 4, core: 2. Of those that a mesh axis runs over, the one named last changes fastest.
Arguments:
- frames: float32 [4, 192, 12288], P('tm', 'pix'), may hold values from 0.05 to 5
- pixel_order: int32 [12288], replicated, may hold values from 0 to 12287, each once
- cycle_sizes: int32 [64], replicated, may hold values from 1 to 384, 12288 in all
- kernel: float32 [5], replicated, may hold values from 0.1 to 1
Outputs:
- correlation: float32 [64, 768, 768], P('pix', 'tm')
The draws below stay inside these ranges and needn't reach their ends.
Inputs may be any that keep to these rules, and one draw needn't show every extreme that they name: `cycle_sizes`: every cycle has one or more pixels, the sizes sum to 12288, and one cycle has exactly 384.
All inputs are finite; a program needn't handle non-finite values.
Results may differ from the reference program's by a relative error of at most 0.00005.
Values sent between devices are 32-bit elements; how exact they have to be, the bound alone decides.
A program may use at most 256 MiB of HBM per device.

```python
import math
import jax
import jax.numpy as jnp
import numpy as np
from jax import lax

CYCLES = 64
TBLK = 192
REACH = 2
PIXELS = 12288
FRAMES = 768
CAP = 384


def level_of(own_key, shape, shards, smallest, high):
    def one(dim, shards_of):
        draws = jax.random.uniform(jax.random.fold_in(jax.random.fold_in(own_key, 6), dim), (shards_of,), jnp.float32, smallest / len(shards), high / len(shards))
        return jnp.repeat(jnp.exp(draws), shape[dim] // shards_of).reshape((-1,) + (1,) * (len(shape) - dim - 1))

    factor_of = one(*shards[0])
    for cut in shards[1:]:
        factor_of = factor_of * one(*cut)
    return factor_of


def split_up(number_of, total, reach, slope):
    loads = [(1 << 20) // math.isqrt(rank ** slope) + 1 for rank in range(2, number_of + 1)]
    rest, given = total - reach - (number_of - 1), [1] * (number_of - 1)
    while rest > 0:
        free = [i for i in range(number_of - 1) if given[i] < reach]
        pool, left = sum([loads[i] for i in free]), rest
        for i in free:
            extra = min(reach - given[i], max(1, left * loads[i] // pool), rest)
            given[i] = given[i] + extra
            rest = rest - extra
    return np.array([reach] + given)


def uneven(stream_key, number_of, total, limit, slope):
    if number_of == 2:
        one = jax.random.randint(stream_key, (), max(1, total - limit), min(limit, total - 1) + 1)
        return jnp.stack([one, total - one])
    tallies = jnp.asarray(split_up(number_of, total, limit, slope), jnp.int32)
    twos = (number_of - 1) // 2
    donor, receiver = tallies[1:1 + 2 * twos:2], tallies[2:2 + 2 * twos:2]
    margin = jnp.minimum(donor - 1, limit - receiver)
    passed = jax.random.randint(jax.random.fold_in(stream_key, 1), (twos,), 0, 1 << 20) % (margin + 1)
    tallies = tallies.at[1:1 + 2 * twos:2].set(donor - passed).at[2:2 + 2 * twos:2].set(receiver + passed)
    return tallies[jax.random.permutation(jax.random.fold_in(stream_key, 2), number_of)]


def setup_inputs(seed: int = 0) -> dict:
    key_list = jax.random.split(jax.random.key(seed), 5)
    return {
        "frames": jnp.clip(jnp.exp(math.log(5.0) - 4.6051702 * jax.random.uniform(key_list[0], (FRAMES // TBLK, TBLK, PIXELS), jnp.float32) ** level_of(key_list[0], (FRAMES // TBLK, TBLK, PIXELS), ((0, 4), (1, 8)), -0.2, 0.2)), 0.05, 5.0),
        "pixel_order": jax.random.permutation(key_list[1], PIXELS).astype(jnp.int32),
        "cycle_sizes": uneven(key_list[2], CYCLES, PIXELS, CAP, 2).astype(jnp.int32),
        "kernel": jnp.clip(jnp.exp(jax.random.uniform(key_list[3], (2 * REACH + 1,), jnp.float32, math.log(0.1), math.log(1.0))), 0.1, 1.0),
    }


def smooth_last(values, kernel):
    count = values.shape[-1]
    padded = jnp.pad(values, ((0, 0), (REACH, REACH)))
    result = kernel[0] * padded[:, 0:count]
    for shift_step in range(1, 2 * REACH + 1):
        result = result + kernel[shift_step] * padded[:, shift_step:shift_step + count]
    return result


def smooth_first(values, kernel):
    count = values.shape[0]
    padded = jnp.pad(values, ((REACH, REACH), (0, 0)))
    result = kernel[0] * padded[0:count]
    for shift_step in range(1, 2 * REACH + 1):
        result = result + kernel[shift_step] * padded[shift_step:shift_step + count]
    return result


def reference(frames, pixel_order, cycle_sizes, kernel):
    series = frames.reshape(FRAMES, PIXELS)
    starts = (jnp.cumsum(cycle_sizes) - cycle_sizes).astype(jnp.int32)
    slots = jnp.arange(CAP, dtype=jnp.int32)
    where_idx = jnp.minimum(starts[:, None] + slots[None, :], PIXELS - 1).astype(jnp.int32)
    valid = slots[None, :] < cycle_sizes[:, None]
    columns = pixel_order[where_idx]

    def one_cycle(packed):
        cols, mask, size = packed
        block = jnp.where(mask[None, :], series[:, cols], 0.0)
        total = jnp.sum(block, axis=1)
        product = jnp.dot(block, block.T, precision=lax.Precision.HIGHEST, preferred_element_type=jnp.float32)
        normed = product * size.astype(jnp.float32) / (total[:, None] * total[None, :])
        return smooth_first(smooth_last(normed, kernel), kernel)

    return lax.map(one_cycle, (columns, valid, cycle_sizes))
```

```python
import functools

import jax
import jax.numpy as jnp
from jax import lax
from jax.experimental import pallas as pl
from jax.experimental.pallas import tpu as pltpu
from jax.sharding import PartitionSpec as P

REACH = 2
LANE = 128
MESH_ID = pl.DeviceIdType.MESH
VMEM_BYTES = 56 * 2**20


def pack_kernel(owned, order, bounds, frames_ref, out_ref, flat, tile, stage):
    group = pl.program_id(0)
    rows, pixels = frames_ref.shape
    slots = out_ref.shape[2]

    @pl.when(group == 0)
    def _():
        tile[...] = jnp.zeros_like(tile)

        @pl.loop(0, pixels // LANE)
        def _(step):
            at = pl.multiple_of(step * LANE, LANE)
            flat[pl.ds(at, LANE), 0:rows] = frames_ref[:, pl.ds(at, LANE)].T

    base = bounds[group * owned]
    count = bounds[(group + 1) * owned] - base
    chunks = (count + LANE - 1) // LANE
    stage[...] = jnp.zeros_like(stage)

    @pl.loop(0, chunks)
    def _(chunk):
        at = pl.multiple_of(chunk * LANE, LANE)
        for u in range(LANE):
            tile[u : u + 1, :] = flat[pl.ds(order[base + at + u], 1), :]
        stage[:, pl.ds(at, LANE)] = tile[...].T[0:rows, :]

    values = stage[...]
    where = lax.broadcasted_iota(jnp.int32, (rows, slots), 1)
    weight = jnp.zeros_like(values)
    for c in range(owned):
        low = bounds[group * owned + c] - base
        high = bounds[group * owned + c + 1] - base
        inside = (where >= low) & (where < high)
        total = jnp.sum(jnp.where(inside, values, 0.0), axis=1, keepdims=True)
        size = jnp.full((rows, 1), (high - low).astype(jnp.float32), jnp.float32)
        weight = jnp.where(inside, jnp.sqrt(size) / total, weight)
    out_ref[0] = jnp.where(weight > 0.0, values, 0.0) * weight


def pack(block, order, bounds, groups, slots):
    rows, pixels = block.shape
    owned = (bounds.shape[0] - 1) // groups
    return pl.pallas_call(
        functools.partial(pack_kernel, owned),
        grid_spec=pltpu.PrefetchScalarGridSpec(
            num_scalar_prefetch=2,
            grid=(groups,),
            in_specs=[pl.BlockSpec((rows, pixels), lambda g, *_: (0, 0))],
            out_specs=pl.BlockSpec((1, rows, slots), lambda g, *_: (g, 0, 0)),
            scratch_shapes=[
                pltpu.VMEM((pixels, LANE), jnp.float32),
                pltpu.VMEM((LANE, LANE), jnp.float32),
                pltpu.VMEM((rows, slots), jnp.float32),
            ],
        ),
        out_shape=jax.ShapeDtypeStruct((groups, rows, slots), jnp.float32),
        compiler_params=pltpu.CompilerParams(vmem_limit_bytes=VMEM_BYTES),
        name="pack",
    )(order, bounds, block)


def spread_kernel(n_pix, n_tm, sent, got, own_sem, pix_send, tm_send, mate_send, recv):
    i = lax.axis_index("pix")
    j = lax.axis_index("tm")
    mate = j + 1 - 2 * lax.rem(j, 2)
    chips = n_tm // 2
    others = [lax.rem(j + 2 * k, n_tm) for k in range(1, chips)]
    peers = [(lax.rem(i + d, n_pix), j) for d in range(1, n_pix)]
    peers += [(i, o) for o in others] + [(i, mate)]
    barrier = pltpu.get_barrier_semaphore()
    for peer in peers:
        pl.semaphore_signal(barrier, inc=1, device_id=peer, device_id_type=MESH_ID)
    pl.semaphore_wait(barrier, len(peers))

    def send(src, slot, send_sem, target):
        return pltpu.make_async_remote_copy(
            src_ref=src,
            dst_ref=got.at[slot],
            send_sem=send_sem,
            recv_sem=recv.at[slot],
            device_id=target,
            device_id_type=MESH_ID,
        )

    def arrived(slot):
        pltpu.make_async_copy(got.at[slot], got.at[slot], recv.at[slot]).wait()

    mine = j * n_pix + i
    started = []
    for d in range(1, n_pix):
        to = lax.rem(i + d, n_pix)
        started.append(send(sent.at[to], mine, pix_send.at[d], (to, j)))
        started[-1].start()
    keep = pltpu.make_async_copy(sent.at[i], got.at[mine], own_sem)
    keep.start()

    for d in range(n_pix):
        source = lax.rem(i + n_pix - d, n_pix)
        slot = j * n_pix + source
        if d:
            arrived(slot)
        src = got.at[slot] if d else sent.at[i]
        for k, other in enumerate(others):
            started.append(send(src, slot, tm_send.at[k * n_pix + d], (i, other)))
            started[-1].start()
        started.append(send(src, slot, mate_send.at[d], (i, mate)))
        started[-1].start()
    for d in range(n_pix):
        source = lax.rem(i + n_pix - d, n_pix)
        for k in range(1, chips):
            slot = lax.rem(j + n_tm - 2 * k, n_tm) * n_pix + source
            arrived(slot)
            started.append(send(got.at[slot], slot, mate_send.at[k * n_pix + d], (i, mate)))
            started[-1].start()
    for d in range(n_pix):
        source = lax.rem(i + n_pix - d, n_pix)
        for k in range(chips):
            arrived(lax.rem(mate + n_tm - 2 * k, n_tm) * n_pix + source)
    keep.wait()
    for copy in started:
        copy.wait_send()


def spread(sent, n_tm, collective_id):
    n_pix, rows, slots = sent.shape
    chips = n_tm // 2
    return pl.pallas_call(
        functools.partial(spread_kernel, n_pix, n_tm),
        in_specs=[pl.BlockSpec(memory_space=pl.ANY)],
        out_specs=pl.BlockSpec(memory_space=pl.ANY),
        out_shape=jax.ShapeDtypeStruct((n_tm * n_pix, rows, slots), jnp.float32),
        scratch_shapes=[
            pltpu.SemaphoreType.DMA,
            pltpu.SemaphoreType.DMA((n_pix,)),
            pltpu.SemaphoreType.DMA((max(1, chips - 1) * n_pix,)),
            pltpu.SemaphoreType.DMA((chips * n_pix,)),
            pltpu.SemaphoreType.DMA((n_tm * n_pix,)),
        ],
        compiler_params=pltpu.CompilerParams(
            collective_id=collective_id, has_side_effects=True
        ),
        name="spread",
    )(sent)


def join_kernel(blocks, window, lows, place, kernel_ref, before, now, after, out_ref, high, low):
    step = pl.program_id(0)
    tblk, slots = now.shape
    frames = high.shape[0]

    @pl.when(step < blocks)
    def _():
        row = lax.broadcasted_iota(jnp.int32, (8, 1), 0)
        top = jnp.where((step > 0) & (row >= 0), 1.0, 0.0)
        end = jnp.where((step < blocks - 1) & (row >= 0), 1.0, 0.0)
        at = pl.multiple_of(step * tblk, tblk)

        @pl.loop(0, slots // LANE)
        def _(c):
            lanes = pl.ds(pl.multiple_of(c * LANE, LANE), LANE)
            wide = jnp.concatenate(
                [before[:, lanes] * top, now[:, lanes], after[:, lanes] * end], axis=0
            )
            smooth = kernel_ref[0] * wide[8 - REACH : 8 - REACH + tblk]
            for k in range(1, 2 * REACH + 1):
                begin = 8 - REACH + k
                smooth = smooth + kernel_ref[k] * wide[begin : begin + tblk]
            rounded = smooth.astype(jnp.bfloat16)
            high[pl.ds(at, tblk), lanes] = rounded
            low[pl.ds(at, tblk), lanes] = (smooth - rounded.astype(jnp.float32)).astype(
                jnp.bfloat16
            )

    @pl.when(step >= blocks)
    def _():
        cycle = step - blocks
        begin = lows[cycle]
        end = lows[cycle + 1]
        at = pl.multiple_of(jnp.minimum(begin // LANE * LANE, slots - window), LANE)
        lanes = pl.ds(at, window)
        rows = pl.ds(pl.multiple_of(place[0] * tblk, tblk), tblk)
        where = lax.broadcasted_iota(jnp.int32, (tblk, window), 1) + at
        inside = (where >= begin) & (where < end)
        mine_high = jnp.where(inside, high[rows, lanes].astype(jnp.float32), 0.0).astype(jnp.bfloat16)
        mine_low = jnp.where(inside, low[rows, lanes].astype(jnp.float32), 0.0).astype(jnp.bfloat16)
        dot = functools.partial(
            lax.dot_general,
            dimension_numbers=(((1,), (1,)), ((), ())),
            preferred_element_type=jnp.float32,
        )
        width = min(768, frames)
        for g in range(0, frames, width):
            all_high = high[g : g + width, lanes]
            all_low = low[g : g + width, lanes]
            small = dot(mine_high, all_low) + dot(mine_low, all_high)
            out_ref[0, :, g : g + width] = small + dot(mine_high, all_high)


def join(series, lows, place, kernel, blocks, cap):
    frames, slots = series.shape
    tblk = frames // blocks
    owned = lows.shape[0] - 1
    window = min(slots, -(-(cap + LANE - 1) // LANE) * LANE)
    eighths = tblk // 8
    edge = frames // 8 - 1
    last = blocks - 1
    return pl.pallas_call(
        functools.partial(join_kernel, blocks, window),
        grid_spec=pltpu.PrefetchScalarGridSpec(
            num_scalar_prefetch=2,
            grid=(blocks + owned,),
            in_specs=[
                pl.BlockSpec(memory_space=pltpu.SMEM),
                pl.BlockSpec(
                    (8, slots), lambda t, *_: (jnp.maximum(jnp.minimum(t, last) * eighths - 1, 0), 0)
                ),
                pl.BlockSpec((tblk, slots), lambda t, *_: (jnp.minimum(t, last), 0)),
                pl.BlockSpec(
                    (8, slots), lambda t, *_: (jnp.minimum((jnp.minimum(t, last) + 1) * eighths, edge), 0)
                ),
            ],
            out_specs=pl.BlockSpec((1, tblk, frames), lambda t, *_: (jnp.maximum(t - blocks, 0), 0, 0)),
            scratch_shapes=[
                pltpu.VMEM((frames, slots), jnp.bfloat16),
                pltpu.VMEM((frames, slots), jnp.bfloat16),
            ],
        ),
        out_shape=jax.ShapeDtypeStruct((owned, tblk, frames), jnp.float32),
        compiler_params=pltpu.CompilerParams(vmem_limit_bytes=VMEM_BYTES),
        name="join",
    )(lows, place, kernel, series, series, series)


def capacities(pixels, groups, limit):
    share = pixels // groups
    listed = [c for c in (share * 4 // 3, share * 3 // 2, share * 5 // 3) if c < limit]
    return [-(-c // LANE) * LANE for c in listed] + [-(-limit // LANE) * LANE]


def per_device(frames, pixel_order, cycle_sizes, kernel):
    block = frames[0]
    pixels = block.shape[1]
    cycles = cycle_sizes.shape[0]
    cap = 2 * pixels // cycles
    n_pix = lax.axis_size("pix")
    n_tm = lax.axis_size("tm")
    owned = cycles // n_pix
    upto = jnp.arange(cycles)[None, :] < jnp.arange(cycles + 1)[:, None]
    bounds = jnp.sum(jnp.where(upto, cycle_sizes[None, :], 0), axis=1).astype(jnp.int32)
    largest = jnp.max(jnp.sum(cycle_sizes.reshape(n_pix, owned), axis=1))
    first = lax.axis_index("pix") * owned
    lows = lax.dynamic_slice_in_dim(bounds, first, owned + 1)
    lows = lows - lows[0]
    place = lax.axis_index("tm").astype(jnp.int32).reshape(1)
    limits = capacities(pixels, n_pix, min(owned * cap, pixels))

    def branch(number, slots):
        def run(block, order, bounds, lows, place, kernel):
            padded = jnp.pad(order, (0, slots))
            sent = pack(block, padded, bounds, n_pix, slots)
            got = spread(sent, n_tm, number + 1)
            return join(got.reshape(-1, slots), lows, place, kernel, n_tm, cap)

        return run

    choice = sum((largest > c).astype(jnp.int32) for c in limits[:-1])
    return lax.switch(
        choice,
        [branch(n, c) for n, c in enumerate(limits)],
        block, pixel_order, bounds, lows, place, kernel,
    )


def solution(mesh):
    placed = (P("tm", "pix", None), P(), P(), P())
    return jax.shard_map(
        per_device, mesh=mesh, in_specs=placed, out_specs=P("pix", "tm", None), check_vma=False
    )
```

```python
import functools

import jax
import jax.numpy as jnp
from jax import lax
from jax.experimental import pallas as pl
from jax.experimental.pallas import tpu as pltpu
from jax.sharding import PartitionSpec as P

REACH = 2
LANE = 128
MESH_ID = pl.DeviceIdType.MESH
VMEM_BYTES = 56 * 2**20


def send_kernel(
    n_pix, n_tm, owned, order, bounds, frames_ref, got, flat, tile, packed,
    own_sem, pix_send, tm_send, mate_send, recv,
):
    rows, pixels = frames_ref.shape
    slots = got.shape[2]
    i = lax.axis_index("pix")
    j = lax.axis_index("tm")
    mate = j + 1 - 2 * lax.rem(j, 2)
    chips = n_tm // 2
    others = [lax.rem(j + 2 * k, n_tm) for k in range(1, chips)]
    peers = [(lax.rem(i + d, n_pix), j) for d in range(1, n_pix)]
    peers += [(i, o) for o in others] + [(i, mate)]
    barrier = pltpu.get_barrier_semaphore()
    for peer in peers:
        pl.semaphore_signal(barrier, inc=1, device_id=peer, device_id_type=MESH_ID)

    tile[...] = jnp.zeros_like(tile)

    @pl.loop(0, pixels // LANE)
    def _(step):
        at = pl.multiple_of(step * LANE, LANE)
        flat[pl.ds(at, LANE), 0:rows] = frames_ref[:, pl.ds(at, LANE)].T

    pl.semaphore_wait(barrier, len(peers))

    def pack(d):
        group = lax.rem(i + d, n_pix)
        base = bounds[group * owned]

        @pl.loop(0, slots // LANE)
        def _(chunk):
            at = pl.multiple_of(chunk * LANE, LANE)
            for u in range(LANE):
                tile[u : u + 1, :] = flat[pl.ds(order[base + at + u], 1), :]
            packed[d, :, pl.ds(at, LANE)] = tile[...].T[0:rows, :]

        values = packed[d]
        where = lax.broadcasted_iota(jnp.int32, (rows, slots), 1)
        weight = jnp.zeros_like(values)
        for c in range(owned):
            low = bounds[group * owned + c] - base
            high = bounds[group * owned + c + 1] - base
            inside = (where >= low) & (where < high)
            total = jnp.sum(jnp.where(inside, values, 0.0), axis=1, keepdims=True)
            size = jnp.full((rows, 1), (high - low).astype(jnp.float32), jnp.float32)
            weight = jnp.where(inside, jnp.sqrt(size) / total, weight)
        packed[d] = values * weight

    def send(src, slot, send_sem, target):
        return pltpu.make_async_remote_copy(
            src_ref=src,
            dst_ref=got.at[slot],
            send_sem=send_sem,
            recv_sem=recv.at[slot],
            device_id=target,
            device_id_type=MESH_ID,
        )

    def arrived(slot):
        pltpu.make_async_copy(got.at[slot], got.at[slot], recv.at[slot]).wait()

    mine = j * n_pix + i
    keep = pltpu.make_async_copy(packed.at[0], got.at[mine], own_sem)

    def over_pix(d):
        return send(packed.at[d], mine, pix_send.at[d], (lax.rem(i + d, n_pix), j))

    def onward(src, slot, d):
        copies = [
            send(src, slot, tm_send.at[k * n_pix + d], (i, other)) for k, other in enumerate(others)
        ]
        return copies + [send(src, slot, mate_send.at[d], (i, mate))]

    def own_frames(d):
        return j * n_pix + lax.rem(i + n_pix - d, n_pix)

    def from_chips(d):
        copies = []
        for k in range(1, chips):
            slot = lax.rem(j + n_tm - 2 * k, n_tm) * n_pix + lax.rem(i + n_pix - d, n_pix)
            copies.append((slot, send(got.at[slot], slot, mate_send.at[k * n_pix + d], (i, mate))))
        return copies

    def pass_on(d):
        slot = own_frames(d)
        arrived(slot)
        for copy in onward(got.at[slot], slot, d):
            copy.start()

    def pass_to_mate(d):
        for slot, copy in from_chips(d):
            arrived(slot)
            copy.start()

    @pl.loop(0, n_pix)
    def _(d):
        pack(d)

        @pl.when(d == 0)
        def _():
            keep.start()
            for copy in onward(packed.at[0], mine, 0):
                copy.start()

        @pl.when(d > 0)
        def _():
            over_pix(d).start()

        @pl.when(d > 1)
        def _():
            pass_on(d - 1)

        @pl.when(d > 2)
        def _():
            pass_to_mate(d - 3)

    pass_on(n_pix - 1)
    for d in range(n_pix - 3, n_pix):
        pass_to_mate(d)
    for d in range(n_pix):
        for k in range(chips):
            arrived(lax.rem(mate + n_tm - 2 * k, n_tm) * n_pix + lax.rem(i + n_pix - d, n_pix))
    keep.wait()
    for d in range(n_pix):
        slot = own_frames(d)
        if d:
            over_pix(d).wait_send()
        for copy in onward(got.at[slot] if d else packed.at[0], slot, d):
            copy.wait_send()
        for _, copy in from_chips(d):
            copy.wait_send()


def pack_and_send(block, order, bounds, n_pix, n_tm, slots, collective_id):
    rows, pixels = block.shape
    owned = (bounds.shape[0] - 1) // n_pix
    chips = n_tm // 2
    return pl.pallas_call(
        functools.partial(send_kernel, n_pix, n_tm, owned),
        in_specs=[
            pl.BlockSpec(memory_space=pltpu.SMEM),
            pl.BlockSpec(memory_space=pltpu.SMEM),
            pl.BlockSpec(memory_space=pltpu.VMEM),
        ],
        out_specs=pl.BlockSpec(memory_space=pl.ANY),
        out_shape=jax.ShapeDtypeStruct((n_tm * n_pix, rows, slots), jnp.float32),
        scratch_shapes=[
            pltpu.VMEM((pixels, LANE), jnp.float32),
            pltpu.VMEM((LANE, LANE), jnp.float32),
            pltpu.VMEM((n_pix, rows, slots), jnp.float32),
            pltpu.SemaphoreType.DMA,
            pltpu.SemaphoreType.DMA((n_pix,)),
            pltpu.SemaphoreType.DMA((max(1, chips - 1) * n_pix,)),
            pltpu.SemaphoreType.DMA((chips * n_pix,)),
            pltpu.SemaphoreType.DMA((n_tm * n_pix,)),
        ],
        compiler_params=pltpu.CompilerParams(
            collective_id=collective_id, has_side_effects=True, vmem_limit_bytes=VMEM_BYTES
        ),
        name="pack_and_send",
    )(order, bounds, block)


def join_kernel(blocks, window, lows, place, kernel_ref, before, now, after, out_ref, high, low):
    step = pl.program_id(0)
    tblk, slots = now.shape
    frames = high.shape[0]

    @pl.when(step < blocks)
    def _():
        row = lax.broadcasted_iota(jnp.int32, (8, 1), 0)
        top = jnp.where((step > 0) & (row >= 0), 1.0, 0.0)
        end = jnp.where((step < blocks - 1) & (row >= 0), 1.0, 0.0)
        at = pl.multiple_of(step * tblk, tblk)

        @pl.loop(0, slots // LANE)
        def _(c):
            lanes = pl.ds(pl.multiple_of(c * LANE, LANE), LANE)
            wide = jnp.concatenate(
                [before[:, lanes] * top, now[:, lanes], after[:, lanes] * end], axis=0
            )
            smooth = kernel_ref[0] * wide[8 - REACH : 8 - REACH + tblk]
            for k in range(1, 2 * REACH + 1):
                begin = 8 - REACH + k
                smooth = smooth + kernel_ref[k] * wide[begin : begin + tblk]
            rounded = smooth.astype(jnp.bfloat16)
            high[pl.ds(at, tblk), lanes] = rounded
            low[pl.ds(at, tblk), lanes] = (smooth - rounded.astype(jnp.float32)).astype(
                jnp.bfloat16
            )

    @pl.when(step >= blocks)
    def _():
        cycle = step - blocks
        begin = lows[cycle]
        end = lows[cycle + 1]
        at = pl.multiple_of(jnp.minimum(begin // LANE * LANE, slots - window), LANE)
        lanes = pl.ds(at, window)
        rows = pl.ds(pl.multiple_of(place[0] * tblk, tblk), tblk)
        where = lax.broadcasted_iota(jnp.int32, (tblk, window), 1) + at
        inside = (where >= begin) & (where < end)
        mine_high = jnp.where(inside, high[rows, lanes].astype(jnp.float32), 0.0).astype(jnp.bfloat16)
        mine_low = jnp.where(inside, low[rows, lanes].astype(jnp.float32), 0.0).astype(jnp.bfloat16)
        dot = functools.partial(
            lax.dot_general,
            dimension_numbers=(((1,), (1,)), ((), ())),
            preferred_element_type=jnp.float32,
        )
        width = min(768, frames)
        for g in range(0, frames, width):
            all_high = high[g : g + width, lanes]
            all_low = low[g : g + width, lanes]
            small = dot(mine_high, all_low) + dot(mine_low, all_high)
            out_ref[0, :, g : g + width] = small + dot(mine_high, all_high)


def join(series, lows, place, kernel, blocks, cap):
    frames, slots = series.shape
    tblk = frames // blocks
    owned = lows.shape[0] - 1
    window = min(slots, -(-(cap + LANE - 1) // LANE) * LANE)
    eighths = tblk // 8
    edge = frames // 8 - 1
    last = blocks - 1
    return pl.pallas_call(
        functools.partial(join_kernel, blocks, window),
        grid_spec=pltpu.PrefetchScalarGridSpec(
            num_scalar_prefetch=2,
            grid=(blocks + owned,),
            in_specs=[
                pl.BlockSpec(memory_space=pltpu.SMEM),
                pl.BlockSpec(
                    (8, slots), lambda t, *_: (jnp.maximum(jnp.minimum(t, last) * eighths - 1, 0), 0)
                ),
                pl.BlockSpec((tblk, slots), lambda t, *_: (jnp.minimum(t, last), 0)),
                pl.BlockSpec(
                    (8, slots), lambda t, *_: (jnp.minimum((jnp.minimum(t, last) + 1) * eighths, edge), 0)
                ),
            ],
            out_specs=pl.BlockSpec((1, tblk, frames), lambda t, *_: (jnp.maximum(t - blocks, 0), 0, 0)),
            scratch_shapes=[
                pltpu.VMEM((frames, slots), jnp.bfloat16),
                pltpu.VMEM((frames, slots), jnp.bfloat16),
            ],
        ),
        out_shape=jax.ShapeDtypeStruct((owned, tblk, frames), jnp.float32),
        compiler_params=pltpu.CompilerParams(vmem_limit_bytes=60 * 2**20),
        name="join",
    )(lows, place, kernel, series, series, series)


def capacities(pixels, groups, limit):
    share = pixels // groups
    listed = [c for c in (share * 4 // 3, share * 3 // 2, share * 5 // 3) if c < limit]
    return [-(-c // LANE) * LANE for c in listed] + [-(-limit // LANE) * LANE]


def per_device(frames, pixel_order, cycle_sizes, kernel):
    block = frames[0]
    pixels = block.shape[1]
    cycles = cycle_sizes.shape[0]
    cap = 2 * pixels // cycles
    n_pix = lax.axis_size("pix")
    n_tm = lax.axis_size("tm")
    owned = cycles // n_pix
    upto = jnp.arange(cycles)[None, :] < jnp.arange(cycles + 1)[:, None]
    bounds = jnp.sum(jnp.where(upto, cycle_sizes[None, :], 0), axis=1).astype(jnp.int32)
    largest = jnp.max(jnp.sum(cycle_sizes.reshape(n_pix, owned), axis=1))
    first = lax.axis_index("pix") * owned
    lows = lax.dynamic_slice_in_dim(bounds, first, owned + 1)
    lows = lows - lows[0]
    place = lax.axis_index("tm").astype(jnp.int32).reshape(1)
    limits = capacities(pixels, n_pix, min(owned * cap, pixels))

    def branch(number, slots):
        def run(block, order, bounds, lows, place, kernel):
            padded = jnp.pad(order, (0, slots))
            got = pack_and_send(block, padded, bounds, n_pix, n_tm, slots, number + 1)
            return join(got.reshape(-1, slots), lows, place, kernel, n_tm, cap)

        return run

    choice = sum((largest > c).astype(jnp.int32) for c in limits[:-1])
    return lax.switch(
        choice,
        [branch(n, c) for n, c in enumerate(limits)],
        block, pixel_order, bounds, lows, place, kernel,
    )


def solution(mesh):
    placed = (P("tm", "pix", None), P(), P(), P())
    return jax.shard_map(
        per_device, mesh=mesh, in_specs=placed, out_specs=P("pix", "tm", None), check_vma=False
    )
```

```python
import functools

import jax
import jax.numpy as jnp
from jax import lax
from jax.experimental import pallas as pl
from jax.experimental.pallas import tpu as pltpu
from jax.sharding import PartitionSpec as P

REACH = 2
LANE = 128
TURNS = 8
LAG = 3
MESH_ID = pl.DeviceIdType.MESH
VMEM_BYTES = 56 * 2**20


def send_kernel(
    n_pix, n_tm, owned, order, bounds, frames_ref, got, flat, packed,
    own_sem, pix_send, tm_send, mate_send, recv,
):
    rows, pixels = frames_ref.shape
    slots = got.shape[2]
    i = lax.axis_index("pix")
    j = lax.axis_index("tm")
    mate = j + 1 - 2 * lax.rem(j, 2)
    chips = n_tm // 2
    others = [lax.rem(j + 2 * k, n_tm) for k in range(1, chips)]
    peers = [(lax.rem(i + d, n_pix), j) for d in range(1, n_pix)]
    peers += [(i, o) for o in others] + [(i, mate)]
    barrier = pltpu.get_barrier_semaphore()
    for peer in peers:
        pl.semaphore_signal(barrier, inc=1, device_id=peer, device_id_type=MESH_ID)

    @pl.loop(0, pixels // LANE // TURNS)
    def _(step):
        for v in range(TURNS):
            at = pl.multiple_of((step * TURNS + v) * LANE, LANE)
            flat[pl.ds(at, LANE), 0:rows] = frames_ref[:, pl.ds(at, LANE)].T

    pl.semaphore_wait(barrier, len(peers))

    def partner(d):
        there, bit = 0, 1
        while bit < n_pix:
            there = there + bit * lax.rem(i // bit + d // bit, 2)
            bit *= 2
        return there

    def order_of(t):
        return t // 2 + n_pix // 2 * (1 - t % 2)

    def pack(d):
        group = partner(d)
        base = bounds[group * owned]

        def chunk(at):
            picked = [
                jnp.concatenate([flat[pl.ds(order[base + at + u + v], 1), :] for v in range(8)], axis=0)
                for u in range(0, LANE, 8)
            ]
            packed[d, :, pl.ds(at, LANE)] = jnp.concatenate(picked, axis=0).T[0:rows, :]

        @pl.loop(0, slots // LANE // 2)
        def _(step):
            for v in range(2):
                chunk(pl.multiple_of((2 * step + v) * LANE, LANE))

        if slots // LANE % 2:
            chunk(slots - LANE)

        values = packed[d]
        where = lax.broadcasted_iota(jnp.int32, (rows, slots), 1)
        weight = jnp.zeros_like(values)
        for c in range(owned):
            low = bounds[group * owned + c] - base
            high = bounds[group * owned + c + 1] - base
            inside = (where >= low) & (where < high)
            total = jnp.sum(jnp.where(inside, values, 0.0), axis=1, keepdims=True)
            size = jnp.full((rows, 1), (high - low).astype(jnp.float32), jnp.float32)
            weight = jnp.where(inside, jnp.sqrt(size) / total, weight)
        packed[d] = values * weight

    def send(src, slot, send_sem, target):
        return pltpu.make_async_remote_copy(
            src_ref=src,
            dst_ref=got.at[slot],
            send_sem=send_sem,
            recv_sem=recv.at[slot],
            device_id=target,
            device_id_type=MESH_ID,
        )

    def arrived(slot):
        pltpu.make_async_copy(got.at[slot], got.at[slot], recv.at[slot]).wait()

    mine = j * n_pix + i
    keep = pltpu.make_async_copy(packed.at[0], got.at[mine], own_sem)

    def over_pix(d):
        return send(packed.at[d], mine, pix_send.at[d], (partner(d), j))

    def onward(src, slot, d):
        copies = [
            send(src, slot, tm_send.at[k * n_pix + d], (i, other)) for k, other in enumerate(others)
        ]
        return copies + [send(src, slot, mate_send.at[d], (i, mate))]

    def own_frames(d):
        return j * n_pix + partner(d)

    def from_chips(d):
        copies = []
        for k in range(1, chips):
            slot = lax.rem(j + n_tm - 2 * k, n_tm) * n_pix + partner(d)
            copies.append((slot, send(got.at[slot], slot, mate_send.at[k * n_pix + d], (i, mate))))
        return copies

    def pass_on(d):
        slot = own_frames(d)
        arrived(slot)
        for copy in onward(got.at[slot], slot, d):
            copy.start()

    def pass_to_mate(d):
        for slot, copy in from_chips(d):
            arrived(slot)
            copy.start()

    @pl.loop(0, n_pix)
    def _(t):
        d = order_of(t)
        pack(d)

        @pl.when(t == 1)
        def _():
            keep.start()
            for copy in onward(packed.at[0], mine, 0):
                copy.start()

        @pl.when(t != 1)
        def _():
            over_pix(d).start()

        @pl.when((t >= LAG) & (t != LAG + 1))
        def _():
            pass_on(order_of(t - LAG))

        @pl.when(t > LAG)
        def _():
            pass_to_mate(order_of(t - LAG - 1))

    for t in range(n_pix - LAG, n_pix + 1):
        if t < n_pix:
            pass_on(order_of(t))
        pass_to_mate(order_of(t - 1))
    for d in range(n_pix):
        for k in range(chips):
            arrived(lax.rem(mate + n_tm - 2 * k, n_tm) * n_pix + partner(d))
    keep.wait()
    for d in range(n_pix):
        slot = own_frames(d)
        if d:
            over_pix(d).wait_send()
        for copy in onward(got.at[slot] if d else packed.at[0], slot, d):
            copy.wait_send()
        for _, copy in from_chips(d):
            copy.wait_send()


def pack_and_send(block, order, bounds, n_pix, n_tm, slots, collective_id):
    rows, pixels = block.shape
    owned = (bounds.shape[0] - 1) // n_pix
    chips = n_tm // 2
    return pl.pallas_call(
        functools.partial(send_kernel, n_pix, n_tm, owned),
        in_specs=[
            pl.BlockSpec(memory_space=pltpu.SMEM),
            pl.BlockSpec(memory_space=pltpu.SMEM),
            pl.BlockSpec(memory_space=pltpu.VMEM),
        ],
        out_specs=pl.BlockSpec(memory_space=pl.ANY),
        out_shape=jax.ShapeDtypeStruct((n_tm * n_pix, rows, slots), jnp.float32),
        scratch_shapes=[
            pltpu.VMEM((pixels, LANE), jnp.float32),
            pltpu.VMEM((n_pix, rows, slots), jnp.float32),
            pltpu.SemaphoreType.DMA,
            pltpu.SemaphoreType.DMA((n_pix,)),
            pltpu.SemaphoreType.DMA((max(1, chips - 1) * n_pix,)),
            pltpu.SemaphoreType.DMA((chips * n_pix,)),
            pltpu.SemaphoreType.DMA((n_tm * n_pix,)),
        ],
        compiler_params=pltpu.CompilerParams(
            collective_id=collective_id, has_side_effects=True, vmem_limit_bytes=VMEM_BYTES
        ),
        name="pack_and_send",
    )(order, bounds, block)


def join_kernel(blocks, window, lows, place, kernel_ref, before, now, after, out_ref, high, low):
    step = pl.program_id(0)
    tblk, slots = now.shape
    frames = high.shape[0]

    @pl.when(step < blocks)
    def _():
        row = lax.broadcasted_iota(jnp.int32, (8, 1), 0)
        top = jnp.where((step > 0) & (row >= 0), 1.0, 0.0)
        end = jnp.where((step < blocks - 1) & (row >= 0), 1.0, 0.0)
        at = pl.multiple_of(step * tblk, tblk)

        @pl.loop(0, slots // LANE)
        def _(c):
            lanes = pl.ds(pl.multiple_of(c * LANE, LANE), LANE)
            wide = jnp.concatenate(
                [before[:, lanes] * top, now[:, lanes], after[:, lanes] * end], axis=0
            )
            smooth = kernel_ref[0] * wide[8 - REACH : 8 - REACH + tblk]
            for k in range(1, 2 * REACH + 1):
                begin = 8 - REACH + k
                smooth = smooth + kernel_ref[k] * wide[begin : begin + tblk]
            rounded = smooth.astype(jnp.bfloat16)
            high[pl.ds(at, tblk), lanes] = rounded
            low[pl.ds(at, tblk), lanes] = (smooth - rounded.astype(jnp.float32)).astype(
                jnp.bfloat16
            )

    @pl.when(step >= blocks)
    def _():
        cycle = step - blocks
        begin = lows[cycle]
        end = lows[cycle + 1]
        at = pl.multiple_of(jnp.minimum(begin // LANE * LANE, slots - window), LANE)
        lanes = pl.ds(at, window)
        rows = pl.ds(pl.multiple_of(place[0] * tblk, tblk), tblk)
        where = lax.broadcasted_iota(jnp.int32, (tblk, window), 1) + at
        inside = (where >= begin) & (where < end)
        mine_high = jnp.where(inside, high[rows, lanes].astype(jnp.float32), 0.0).astype(jnp.bfloat16)
        mine_low = jnp.where(inside, low[rows, lanes].astype(jnp.float32), 0.0).astype(jnp.bfloat16)
        dot = functools.partial(
            lax.dot_general,
            dimension_numbers=(((1,), (1,)), ((), ())),
            preferred_element_type=jnp.float32,
        )
        width = min(768, frames)
        for g in range(0, frames, width):
            all_high = high[g : g + width, lanes]
            all_low = low[g : g + width, lanes]
            small = dot(mine_high, all_low) + dot(mine_low, all_high)
            out_ref[0, :, g : g + width] = small + dot(mine_high, all_high)


def join(series, lows, place, kernel, blocks, cap):
    frames, slots = series.shape
    tblk = frames // blocks
    owned = lows.shape[0] - 1
    window = min(slots, -(-(cap + LANE - 1) // LANE) * LANE)
    eighths = tblk // 8
    edge = frames // 8 - 1
    last = blocks - 1
    return pl.pallas_call(
        functools.partial(join_kernel, blocks, window),
        grid_spec=pltpu.PrefetchScalarGridSpec(
            num_scalar_prefetch=2,
            grid=(blocks + owned,),
            in_specs=[
                pl.BlockSpec(memory_space=pltpu.SMEM),
                pl.BlockSpec(
                    (8, slots), lambda t, *_: (jnp.maximum(jnp.minimum(t, last) * eighths - 1, 0), 0)
                ),
                pl.BlockSpec((tblk, slots), lambda t, *_: (jnp.minimum(t, last), 0)),
                pl.BlockSpec(
                    (8, slots), lambda t, *_: (jnp.minimum((jnp.minimum(t, last) + 1) * eighths, edge), 0)
                ),
            ],
            out_specs=pl.BlockSpec((1, tblk, frames), lambda t, *_: (jnp.maximum(t - blocks, 0), 0, 0)),
            scratch_shapes=[
                pltpu.VMEM((frames, slots), jnp.bfloat16),
                pltpu.VMEM((frames, slots), jnp.bfloat16),
            ],
        ),
        out_shape=jax.ShapeDtypeStruct((owned, tblk, frames), jnp.float32),
        compiler_params=pltpu.CompilerParams(vmem_limit_bytes=60 * 2**20),
        name="join",
    )(lows, place, kernel, series, series, series)


def capacities(pixels, groups, limit):
    share = pixels // groups
    listed = [c for c in range(share * 7 // 6, share * 5 // 3 + 1, LANE) if c < limit]
    return [-(-c // LANE) * LANE for c in listed] + [-(-limit // LANE) * LANE]


def per_device(frames, pixel_order, cycle_sizes, kernel):
    block = frames[0]
    pixels = block.shape[1]
    cycles = cycle_sizes.shape[0]
    cap = 2 * pixels // cycles
    n_pix = lax.axis_size("pix")
    n_tm = lax.axis_size("tm")
    owned = cycles // n_pix
    upto = jnp.arange(cycles)[None, :] < jnp.arange(cycles + 1)[:, None]
    bounds = jnp.sum(jnp.where(upto, cycle_sizes[None, :], 0), axis=1).astype(jnp.int32)
    largest = jnp.max(jnp.sum(cycle_sizes.reshape(n_pix, owned), axis=1))
    first = lax.axis_index("pix") * owned
    lows = lax.dynamic_slice_in_dim(bounds, first, owned + 1)
    lows = lows - lows[0]
    place = lax.axis_index("tm").astype(jnp.int32).reshape(1)
    limits = capacities(pixels, n_pix, min(owned * cap, pixels))

    def branch(number, slots):
        def run(block, order, bounds, lows, place, kernel):
            padded = jnp.pad(order, (0, slots))
            got = pack_and_send(block, padded, bounds, n_pix, n_tm, slots, number + 1)
            return join(got.reshape(-1, slots), lows, place, kernel, n_tm, cap)

        return run

    choice = sum((largest > c).astype(jnp.int32) for c in limits[:-1])
    return lax.switch(
        choice,
        [branch(n, c) for n, c in enumerate(limits)],
        block, pixel_order, bounds, lows, place, kernel,
    )


def solution(mesh):
    placed = (P("tm", "pix", None), P(), P(), P())
    return jax.shard_map(
        per_device, mesh=mesh, in_specs=placed, out_specs=P("pix", "tm", None), check_vma=False
    )
```

```python
import functools

import jax
import jax.numpy as jnp
from jax import lax
from jax.experimental import pallas as pl
from jax.experimental.pallas import tpu as pltpu
from jax.sharding import PartitionSpec as P

REACH = 2
LANE = 128
TURNS = 8
LAG = 3
MESH_ID = pl.DeviceIdType.MESH
VMEM_BYTES = 56 * 2**20


def send_kernel(
    n_pix, n_tm, owned, order, bounds, frames_ref, got, flat, packed,
    own_sem, pix_send, tm_send, mate_send, recv,
):
    rows, pixels = frames_ref.shape
    slots = got.shape[2]
    i = lax.axis_index("pix")
    j = lax.axis_index("tm")
    mate = j + 1 - 2 * lax.rem(j, 2)
    chips = n_tm // 2
    others = [lax.rem(j + 2 * k, n_tm) for k in range(1, chips)]
    peers = [(lax.rem(i + d, n_pix), j) for d in range(1, n_pix)]
    peers += [(i, o) for o in others] + [(i, mate)]
    barrier = pltpu.get_barrier_semaphore()
    for peer in peers:
        pl.semaphore_signal(barrier, inc=1, device_id=peer, device_id_type=MESH_ID)

    @pl.loop(0, pixels // LANE // TURNS)
    def _(step):
        for v in range(TURNS):
            at = pl.multiple_of((step * TURNS + v) * LANE, LANE)
            flat[pl.ds(at, LANE), 0:rows] = frames_ref[:, pl.ds(at, LANE)].T

    pl.semaphore_wait(barrier, len(peers))

    def partner(d):
        there, bit = 0, 1
        while bit < n_pix:
            there = there + bit * lax.rem(i // bit + d // bit, 2)
            bit *= 2
        return there

    def order_of(t):
        return t // 2 + n_pix // 2 * (1 - t % 2)

    def pack(d):
        group = partner(d)
        base = bounds[group * owned]

        def chunk(at):
            picked = [
                jnp.concatenate([flat[pl.ds(order[base + at + u + v], 1), :] for v in range(8)], axis=0)
                for u in range(0, LANE, 8)
            ]
            packed[d, :, pl.ds(at, LANE)] = jnp.concatenate(picked, axis=0).T[0:rows, :]

        @pl.loop(0, slots // LANE // 2)
        def _(step):
            for v in range(2):
                chunk(pl.multiple_of((2 * step + v) * LANE, LANE))

        if slots // LANE % 2:
            chunk(slots - LANE)

        values = packed[d]
        where = lax.broadcasted_iota(jnp.int32, (rows, slots), 1)
        weight = jnp.zeros_like(values)
        for c in range(owned):
            low = bounds[group * owned + c] - base
            high = bounds[group * owned + c + 1] - base
            inside = (where >= low) & (where < high)
            total = jnp.sum(jnp.where(inside, values, 0.0), axis=1, keepdims=True)
            size = jnp.full((rows, 1), (high - low).astype(jnp.float32), jnp.float32)
            weight = jnp.where(inside, jnp.sqrt(size) / total, weight)
        packed[d] = values * weight

    def send(src, slot, send_sem, target):
        return pltpu.make_async_remote_copy(
            src_ref=src,
            dst_ref=got.at[slot],
            send_sem=send_sem,
            recv_sem=recv.at[slot],
            device_id=target,
            device_id_type=MESH_ID,
        )

    def arrived(slot):
        pltpu.make_async_copy(got.at[slot], got.at[slot], recv.at[slot]).wait()

    mine = j * n_pix + i
    keep = pltpu.make_async_copy(packed.at[0], got.at[mine], own_sem)

    def over_pix(d):
        return send(packed.at[d], mine, pix_send.at[d], (partner(d), j))

    def onward(src, slot, d):
        copies = [
            send(src, slot, tm_send.at[k * n_pix + d], (i, other)) for k, other in enumerate(others)
        ]
        return copies + [send(src, slot, mate_send.at[d], (i, mate))]

    def own_frames(d):
        return j * n_pix + partner(d)

    def from_chips(d):
        copies = []
        for k in range(1, chips):
            slot = lax.rem(j + n_tm - 2 * k, n_tm) * n_pix + partner(d)
            copies.append((slot, send(got.at[slot], slot, mate_send.at[k * n_pix + d], (i, mate))))
        return copies

    def pass_on(d):
        slot = own_frames(d)
        arrived(slot)
        for copy in onward(got.at[slot], slot, d):
            copy.start()

    def pass_to_mate(d):
        for slot, copy in from_chips(d):
            arrived(slot)
            copy.start()

    @pl.loop(0, n_pix)
    def _(t):
        d = order_of(t)
        pack(d)

        @pl.when(t == 1)
        def _():
            keep.start()
            for copy in onward(packed.at[0], mine, 0):
                copy.start()

        @pl.when(t != 1)
        def _():
            over_pix(d).start()

        @pl.when((t >= LAG) & (t != LAG + 1))
        def _():
            pass_on(order_of(t - LAG))

        @pl.when(t > LAG)
        def _():
            pass_to_mate(order_of(t - LAG - 1))

    for t in range(n_pix - LAG, n_pix + 1):
        if t < n_pix:
            pass_on(order_of(t))
        pass_to_mate(order_of(t - 1))
    for d in range(n_pix):
        for k in range(chips):
            arrived(lax.rem(mate + n_tm - 2 * k, n_tm) * n_pix + partner(d))
    keep.wait()
    for d in range(n_pix):
        slot = own_frames(d)
        if d:
            over_pix(d).wait_send()
        for copy in onward(got.at[slot] if d else packed.at[0], slot, d):
            copy.wait_send()
        for _, copy in from_chips(d):
            copy.wait_send()


def pack_and_send(block, order, bounds, n_pix, n_tm, slots, collective_id):
    rows, pixels = block.shape
    owned = (bounds.shape[0] - 1) // n_pix
    chips = n_tm // 2
    return pl.pallas_call(
        functools.partial(send_kernel, n_pix, n_tm, owned),
        in_specs=[
            pl.BlockSpec(memory_space=pltpu.SMEM),
            pl.BlockSpec(memory_space=pltpu.SMEM),
            pl.BlockSpec(memory_space=pltpu.VMEM),
        ],
        out_specs=pl.BlockSpec(memory_space=pl.ANY),
        out_shape=jax.ShapeDtypeStruct((n_tm * n_pix, rows, slots), jnp.float32),
        scratch_shapes=[
            pltpu.VMEM((pixels, LANE), jnp.float32),
            pltpu.VMEM((n_pix, rows, slots), jnp.float32),
            pltpu.SemaphoreType.DMA,
            pltpu.SemaphoreType.DMA((n_pix,)),
            pltpu.SemaphoreType.DMA((max(1, chips - 1) * n_pix,)),
            pltpu.SemaphoreType.DMA((chips * n_pix,)),
            pltpu.SemaphoreType.DMA((n_tm * n_pix,)),
        ],
        compiler_params=pltpu.CompilerParams(
            collective_id=collective_id, has_side_effects=True, vmem_limit_bytes=VMEM_BYTES
        ),
        name="pack_and_send",
    )(order, bounds, block)


def join_kernel(blocks, window, lows, place, kernel_ref, before, now, after, out_ref, high, low):
    step = pl.program_id(0)
    tblk, slots = now.shape
    frames = high.shape[0]

    @pl.when(step < blocks)
    def _():
        row = lax.broadcasted_iota(jnp.int32, (8, 1), 0)
        top = jnp.where((step > 0) & (row >= 0), 1.0, 0.0)
        end = jnp.where((step < blocks - 1) & (row >= 0), 1.0, 0.0)
        at = pl.multiple_of(step * tblk, tblk)

        @pl.loop(0, slots // LANE)
        def _(c):
            lanes = pl.ds(pl.multiple_of(c * LANE, LANE), LANE)
            wide = jnp.concatenate(
                [before[:, lanes] * top, now[:, lanes], after[:, lanes] * end], axis=0
            )
            smooth = kernel_ref[0] * wide[8 - REACH : 8 - REACH + tblk]
            for k in range(1, 2 * REACH + 1):
                begin = 8 - REACH + k
                smooth = smooth + kernel_ref[k] * wide[begin : begin + tblk]
            rounded = smooth.astype(jnp.bfloat16)
            high[pl.ds(at, tblk), lanes] = rounded
            low[pl.ds(at, tblk), lanes] = (smooth - rounded.astype(jnp.float32)).astype(
                jnp.bfloat16
            )

    @pl.when(step >= blocks)
    def _():
        cycle = step - blocks
        begin = lows[cycle]
        end = lows[cycle + 1]
        at = pl.multiple_of(jnp.minimum(begin // LANE * LANE, slots - window), LANE)
        lanes = pl.ds(at, window)
        rows = pl.ds(pl.multiple_of(place[0] * tblk, tblk), tblk)
        where = lax.broadcasted_iota(jnp.int32, (tblk, window), 1) + at
        inside = (where >= begin) & (where < end)
        mine_high = jnp.where(inside, high[rows, lanes].astype(jnp.float32), 0.0).astype(jnp.bfloat16)
        mine_low = jnp.where(inside, low[rows, lanes].astype(jnp.float32), 0.0).astype(jnp.bfloat16)
        mine = jnp.concatenate([mine_high, mine_low], axis=0)
        dot = functools.partial(
            lax.dot_general,
            dimension_numbers=(((1,), (1,)), ((), ())),
            preferred_element_type=jnp.float32,
        )
        width = min(768, frames)
        for g in range(0, frames, width):
            all_high = high[g : g + width, lanes]
            all_low = low[g : g + width, lanes]
            both = dot(mine, all_high)
            small = dot(mine_high, all_low) + both[tblk:]
            out_ref[0, :, g : g + width] = small + both[:tblk]


def join(series, lows, place, kernel, blocks, cap):
    frames, slots = series.shape
    tblk = frames // blocks
    owned = lows.shape[0] - 1
    window = min(slots, -(-(cap + LANE - 1) // LANE) * LANE)
    eighths = tblk // 8
    edge = frames // 8 - 1
    last = blocks - 1
    return pl.pallas_call(
        functools.partial(join_kernel, blocks, window),
        grid_spec=pltpu.PrefetchScalarGridSpec(
            num_scalar_prefetch=2,
            grid=(blocks + owned,),
            in_specs=[
                pl.BlockSpec(memory_space=pltpu.SMEM),
                pl.BlockSpec(
                    (8, slots), lambda t, *_: (jnp.maximum(jnp.minimum(t, last) * eighths - 1, 0), 0)
                ),
                pl.BlockSpec((tblk, slots), lambda t, *_: (jnp.minimum(t, last), 0)),
                pl.BlockSpec(
                    (8, slots), lambda t, *_: (jnp.minimum((jnp.minimum(t, last) + 1) * eighths, edge), 0)
                ),
            ],
            out_specs=pl.BlockSpec((1, tblk, frames), lambda t, *_: (jnp.maximum(t - blocks, 0), 0, 0)),
            scratch_shapes=[
                pltpu.VMEM((frames, slots), jnp.bfloat16),
                pltpu.VMEM((frames, slots), jnp.bfloat16),
            ],
        ),
        out_shape=jax.ShapeDtypeStruct((owned, tblk, frames), jnp.float32),
        compiler_params=pltpu.CompilerParams(vmem_limit_bytes=60 * 2**20),
        name="join",
    )(lows, place, kernel, series, series, series)


def capacities(pixels, groups, limit):
    share = pixels // groups
    listed = [c for c in range(share * 7 // 6, share * 5 // 3 + 1, LANE) if c < limit]
    return [-(-c // LANE) * LANE for c in listed] + [-(-limit // LANE) * LANE]


def per_device(frames, pixel_order, cycle_sizes, kernel):
    block = frames[0]
    pixels = block.shape[1]
    cycles = cycle_sizes.shape[0]
    cap = 2 * pixels // cycles
    n_pix = lax.axis_size("pix")
    n_tm = lax.axis_size("tm")
    owned = cycles // n_pix
    upto = jnp.arange(cycles)[None, :] < jnp.arange(cycles + 1)[:, None]
    bounds = jnp.sum(jnp.where(upto, cycle_sizes[None, :], 0), axis=1).astype(jnp.int32)
    group = jnp.arange(cycles)[None, :] // owned == jnp.arange(n_pix)[:, None]
    largest = jnp.max(jnp.sum(jnp.where(group, cycle_sizes[None, :], 0), axis=1))
    first = lax.axis_index("pix") * owned
    lows = lax.dynamic_slice_in_dim(bounds, first, owned + 1)
    lows = lows - lows[0]
    place = lax.axis_index("tm").astype(jnp.int32).reshape(1)
    limits = capacities(pixels, n_pix, min(owned * cap, pixels))

    def branch(number, slots):
        def run(block, order, bounds, lows, place, kernel):
            padded = jnp.pad(order, (0, slots))
            got = pack_and_send(block, padded, bounds, n_pix, n_tm, slots, number + 1)
            return join(got.reshape(-1, slots), lows, place, kernel, n_tm, cap)

        return run

    choice = jnp.sum((largest > jnp.array(limits[:-1], jnp.int32)).astype(jnp.int32))
    return lax.switch(
        choice,
        [branch(n, c) for n, c in enumerate(limits)],
        block, pixel_order, bounds, lows, place, kernel,
    )


def solution(mesh):
    placed = (P("tm", "pix", None), P(), P(), P())
    return jax.shard_map(
        per_device, mesh=mesh, in_specs=placed, out_specs=P("pix", "tm", None), check_vma=False
    )
```
